256 devices in a mesh: inter: 16 (over x, y), intra: 16 (over z, core).
Axes of the slice: x: 4, y: 4, z: 8, core: 2. Of those that a mesh axis runs over, the one named last changes fastest.
Arguments:
- activations: bfloat16 [131072, 512], P(('inter', 'intra')), may hold values from -24 to 24
- cotangent: bfloat16 [131072, 5120], P(('inter', 'intra')), may hold values from -6 to 6
- counts: int32 [16, 16], P('inter', 'intra'), may hold values from 1 to 4, as said below
- dither_rows: int32 [16, 512], P('inter'), may hold values from 0 to 255
- dither_cols: int32 [16, 5120], P('inter'), may hold values from 0 to 255
- sign_bits: int32 [5120], replicated, may hold values from 0 to 1
Outputs:
- synced: float32 [512, 5120], P('inter')
The draws below stay inside these ranges and needn't reach their ends.
Inputs may be any that keep to these rules, and one draw needn't show every extreme that they name: Each device processes counts of its 4 microbatch slots; some device has 4 and some device has one in every draw.
All inputs are finite; a program needn't handle non-finite values.
Results may differ from the reference program's by a relative error of at most 0.0003.
Values sent between devices are 32-bit elements; how exact they have to be, the bound alone decides.
A program may use at most 128 MiB of HBM per device.

```python
import math
import jax
import jax.numpy as jnp
from jax import lax

D = 5120
FFS = 512
HBLK = 256
MB = 128
MB_MAX = 4
TOKENS = 131072
N_INTER = 16
N_INTRA = 16


def draw_counts(key, part):
    key = jax.random.fold_in(key, 7)
    first, second, third = jax.random.split(key, 3)
    total_devices = N_INTER * N_INTRA
    base = jax.random.randint(first, (N_INTER, N_INTRA), 0, 10)
    higher = jax.random.randint(second, (N_INTER, N_INTRA), 2, MB_MAX + 1)
    values = jnp.where(base < 6, 1, higher)
    position = jax.random.randint(third, (), 0, total_devices)
    flat = jnp.arange(total_devices, dtype=jnp.int32).reshape(N_INTER, N_INTRA)
    values = jnp.where(flat == position, MB_MAX, values)
    values = jnp.where(flat == (position + 1) % total_devices, 1, values)
    return values.astype(jnp.int32)


def with_ends(entries, own_key, smallest, high):
    longest = entries.shape.index(max(entries.shape))
    spots = []
    for shift in (0, 1):
        where = [jax.random.randint(jax.random.fold_in(own_key, axis), (), 0, length) for axis, length in enumerate(entries.shape)]
        where[longest] = (where[longest] + shift) % entries.shape[longest]
        spots.append(tuple(where))
    return entries.at[spots[0]].set(smallest).at[spots[1]].set(high)


def raised(array, own_key, source, target, blocks, factor):
    owner, partner = [(jnp.arange(array.shape[dim]) // (array.shape[dim] // blocks)).reshape([-1 if axis == dim else 1 for axis in range(array.ndim)]) for dim in (source, target)]
    chosen = jax.random.permutation(own_key, blocks)[partner]
    strong = (owner == chosen) | (owner == (partner + blocks // 2) % blocks)
    return jnp.where(strong, factor * array, array)


def levels(key, dims, pieces, least, largest):
    factor_of, own = 1.0, jax.random.fold_in(key, 6)
    for axis_at, shards_of in pieces:
        heights = jnp.exp(jax.random.uniform(jax.random.fold_in(own, axis_at), (shards_of,), jnp.float32, least / len(pieces), largest / len(pieces)))
        factor_of = factor_of * jnp.repeat(heights, dims[axis_at] // shards_of).reshape([-1 if axis == axis_at else 1 for axis in range(len(dims))])
    return factor_of


def normal_values(key, dims, scale, limit, pieces=(), held_as=jnp.bfloat16):
    entries = jax.random.normal(key, dims, jnp.float32) * scale
    if len(pieces) > 0:
        entries = levels(key, dims, pieces, -0.22, 0.18) * entries
    return jnp.clip(entries, min=-limit, max=limit).astype(held_as)


def noise_with(stream_key, shape, deviation, reach, cuts, heavy, kind=jnp.bfloat16):
    values = deviation * jax.random.normal(stream_key, shape, jnp.float32)
    if cuts:
        values = values * levels(stream_key, shape, cuts, -0.22, 0.18)
    return jnp.clip(raised(values, jax.random.fold_in(stream_key, 3), *heavy), -reach, reach).astype(kind)


def setup_inputs(seed: int = 0) -> dict:
    seeds = jax.random.split(jax.random.key(seed), 7)
    return {
        "activations": noise_with(seeds[0], (TOKENS, FFS), 1.0, 24.0, ((0, 256),), (0, 1, 256, 6.0)),
        "cotangent": normal_values(seeds[1], (TOKENS, D), 1.0, 6.0, ((0, 256),)),
        "counts": draw_counts(jax.random.fold_in(seeds[6], 71), 0),
        "dither_rows": with_ends(jax.random.randint(seeds[3], (N_INTER, FFS), 0, 256), jax.random.fold_in(seeds[3], 1), 0, 255).astype(jnp.int32),
        "dither_cols": with_ends(jax.random.randint(seeds[4], (N_INTER, D), 0, 256), jax.random.fold_in(seeds[4], 1), 0, 255).astype(jnp.int32),
        "sign_bits": with_ends(jax.random.randint(seeds[5], (D,), 0, 2), jax.random.fold_in(seeds[5], 1), 0, 1).astype(jnp.int32),
    }


def sylvester(block_len):
    first = jnp.arange(block_len, dtype=jnp.int32)
    parity = jnp.zeros((block_len, block_len), jnp.int32)
    for level in range(block_len.bit_length() - 1):
        parity = parity + first[:, None] // 2 ** level % 2 * (first[None, :] // 2 ** level % 2)
    return (1 - 2 * (parity % 2)).astype(jnp.float32)

def rotate_blocks(field, signs_float, hadamard):
    row_count = field.shape[0]
    col_count = field.shape[1]
    block_len = hadamard.shape[0]
    blocks = (field * signs_float).reshape(row_count, col_count // block_len, block_len)
    turned = jnp.einsum('rbk,kl->rbl', blocks, hadamard, precision=lax.Precision.HIGHEST) / math.sqrt(block_len)
    return turned.reshape(row_count, col_count)

def unrotate_blocks(field, signs_float, hadamard):
    row_count = field.shape[0]
    col_count = field.shape[1]
    block_len = hadamard.shape[0]
    blocks = field.reshape(row_count, col_count // block_len, block_len)
    turned = jnp.einsum('rbk,kl->rbl', blocks, hadamard, precision=lax.Precision.HIGHEST) / math.sqrt(block_len)
    return turned.reshape(row_count, col_count) * signs_float

def make_dither(row_terms, col_terms):
    joined = (row_terms[:, None] + col_terms[None, :]) % 256
    return (joined.astype(jnp.float32) + 0.5) / 256.0 - 0.5

def block_peaks(rotated, block_len):
    row_count = rotated.shape[0]
    col_count = rotated.shape[1]
    return lax.optimization_barrier(jnp.max(jnp.abs(rotated).reshape(row_count, col_count // block_len, block_len), axis=-1))

def encode(rotated, scale, dither):
    row_count = rotated.shape[0]
    col_count = rotated.shape[1]
    nblocks = scale.shape[1]
    scaled = (rotated.reshape(row_count, nblocks, col_count // nblocks) / scale[..., None] * 7.5).reshape(row_count, col_count)
    shifted = scaled + dither
    return shifted - jnp.sin(2.0 * math.pi * shifted) / (2.0 * math.pi) - dither

def decode(sums, scale):
    row_count = sums.shape[0]
    col_count = sums.shape[1]
    nblocks = scale.shape[1]
    return (sums.reshape(row_count, nblocks, col_count // nblocks) * (scale / 7.5)[..., None]).reshape(row_count, col_count)

def reference(activations, cotangent, counts, dither_rows, dither_cols, sign_bits):
    hadamard = sylvester(HBLK)
    signs_float = (1 - 2 * sign_bits).astype(jnp.float32)
    slots = MB * MB_MAX
    acts_all = activations.reshape(N_INTER, N_INTRA, slots, FFS)
    cots_all = cotangent.reshape(N_INTER, N_INTRA, slots, D)

    def pod_column(running, column):

        def member(member_index):
            acts_dev = acts_all[member_index, column]
            cots_dev = cots_all[member_index, column]
            amount = counts[member_index, column]

            def accumulate(step, partial_sum):
                left = lax.dynamic_slice_in_dim(acts_dev, step * MB, MB, 0)
                right = lax.dynamic_slice_in_dim(cots_dev, step * MB, MB, 0)
                return partial_sum + lax.dot_general(left, right, (((0,), (0,)), ((), ())), preferred_element_type=jnp.float32)
            gradient = lax.fori_loop(0, amount, accumulate, jnp.zeros((FFS, D), jnp.float32))
            gradient = gradient * lax.rsqrt((MB * amount).astype(jnp.float32))
            return rotate_blocks(gradient, signs_float, hadamard)
        rotated = lax.map(member, jnp.arange(N_INTER, dtype=jnp.int32))
        peaks = jax.vmap(lambda one: block_peaks(one, HBLK))(rotated)
        scale = lax.optimization_barrier(jnp.max(peaks, axis=0)) + 1e-06

        def coded(member_index):
            dither = make_dither(dither_rows[member_index], dither_cols[member_index])
            return encode(rotated[member_index], scale, dither)
        sums = lax.optimization_barrier(jnp.sum(lax.map(coded, jnp.arange(N_INTER, dtype=jnp.int32)), axis=0))
        return (running + decode(sums, scale), None)
    total, _ = lax.scan(pod_column, jnp.zeros((FFS, D), jnp.float32), jnp.arange(N_INTRA, dtype=jnp.int32))
    return unrotate_blocks(total, signs_float, hadamard) * (1.0 / math.sqrt(N_INTER * N_INTRA))
```

```python
import math

import jax
import jax.numpy as jnp
from jax import lax
from jax.experimental import pallas as pl
from jax.experimental.pallas import tpu as pltpu
from jax.sharding import PartitionSpec as P

F32 = jnp.float32
BF16 = jnp.bfloat16
HBLK = 256
MB = 128
SIDE = 4
CORES = 2
GROUP = 4
SINE = (
    6.283182621002197,
    -41.34142303466797,
    81.59618377685547,
    -76.5801010131836,
    41.20538330078125,
    -12.27124309539795,
)


def make_kernel(depth, groups):
    cols = groups * GROUP * HBLK

    def kernel(
        counts, drows, dcols, signs, a_hbm, c_hbm, out,
        cbuf, abuf, a2, hmat, colterm, rowterm, rot, pk1, pk2, scl,
        rpx, rpy, rcore, ra, rb, ra2, rb2, stage2, shares, rz, gathered,
        load_sem, s_pk, r_px, r_py, s_core, r_core, s_one, r_a, r_b,
        s_two, r_a2, r_b2, s_z, r_z, s_out, r_out,
    ):
        i_me = lax.axis_index("inter")
        j_me = lax.axis_index("intra")
        x, y = i_me // SIDE, i_me % SIDE
        z, core = j_me // CORES, j_me % CORES
        other = 1 - core

        def at_x(u):
            return (lax.rem(x + u, SIDE) * SIDE + y, j_me)

        def at_y(u):
            return (x * SIDE + lax.rem(y + u, SIDE), j_me)

        def along(axis, u):
            return at_x(u) if axis == 0 else at_y(u)

        def at_z(u, c):
            return (i_me, lax.rem(z + u, depth) * CORES + c)

        sibling = at_z(0, other)

        def put(src, dst, send, recv, device):
            pltpu.make_async_remote_copy(
                src_ref=src, dst_ref=dst, send_sem=send, recv_sem=recv,
                device_id=device, device_id_type=pl.DeviceIdType.MESH,
            ).start()

        def wait_for(ref, sem):
            pltpu.make_async_copy(ref, ref, sem).wait()

        barrier = pltpu.get_barrier_semaphore()
        peers = [at_x(u) for u in range(1, SIDE)] + [at_y(u) for u in range(1, SIDE)]
        peers += [at_z(u, c) for u in range(1, depth) for c in range(CORES)] + [sibling]
        for device in peers:
            pl.semaphore_signal(
                barrier, inc=1, device_id=device, device_id_type=pl.DeviceIdType.MESH
            )

        load_a = pltpu.make_async_copy(a_hbm, abuf, load_sem.at[groups])
        load_a.start()
        width = GROUP * HBLK

        def load_c(g):
            return pltpu.make_async_copy(
                c_hbm.at[:, pl.ds(pl.multiple_of(g * width, width), width)],
                cbuf.at[g], load_sem.at[g],
            )

        for g in range(groups):
            load_c(g).start()

        first = lax.broadcasted_iota(jnp.int32, (HBLK, HBLK), 0)
        second = lax.broadcasted_iota(jnp.int32, (HBLK, HBLK), 1)
        both = first & second
        both = both ^ (both >> 4)
        both = both ^ (both >> 2)
        both = both ^ (both >> 1)
        hmat[...] = (1 - 2 * (both & 1)).astype(F32)

        def turn(tile, carry):
            row = dcols[:, pl.ds(pl.multiple_of(tile * 128, 128), 128)].astype(F32) * (1.0 / 256.0)
            colterm[pl.ds(pl.multiple_of(tile * 128, 128), 128), :] = jnp.broadcast_to(
                row, (128, 128)
            ).T
            return carry

        lax.fori_loop(0, cols // 128, turn, 0)

        load_a.wait()
        amount = counts[0, 0]
        hidden = abuf.shape[1]
        token = lax.broadcasted_iota(jnp.int32, abuf.shape, 0)
        a2[0] = jnp.where(token < amount * MB, abuf[...].astype(F32), 0.0).astype(BF16)
        sub = hidden // (SIDE * SIDE)
        to = lax.broadcasted_iota(jnp.int32, (hidden, hidden), 1)
        source = (to // sub % SIDE) * (SIDE * sub) + to // (SIDE * sub) * sub + to % sub
        fro = lax.broadcasted_iota(jnp.int32, (hidden, hidden), 0)
        order = jnp.where(fro == source, 1.0, 0.0).astype(BF16)
        a2[1] = jnp.dot(a2[0], order, preferred_element_type=F32).astype(BF16)
        row_ints = jnp.broadcast_to(drows[...].astype(F32), (8, hidden))
        rowterm[0] = (row_ints + 0.5) * (1.0 / 256.0)
        row_ints = jnp.dot(row_ints.astype(BF16), order, preferred_element_type=F32)
        rowterm[1] = (row_ints + 0.5) * (1.0 / 256.0)

        counted = jnp.full((1, hidden), amount, jnp.int32)
        weight = jnp.where(counted == 1, 1.0 / math.sqrt(MB), 1.0 / math.sqrt(2 * MB))
        weight = jnp.where(counted == 3, 1.0 / math.sqrt(3 * MB), weight)
        weight = jnp.where(counted == 4, 1.0 / math.sqrt(4 * MB), weight)
        weight = weight * (1.0 / math.sqrt(HBLK))

        def signed(block):
            return (hmat[...] * signs[pl.ds(block, 1), :]).astype(BF16)

        def split(value):
            high = value.astype(BF16)
            return high, (value - high.astype(F32)).astype(BF16)

        def rotate(g):
            load_c(g).wait()
            peaks = []
            for k in range(GROUP):
                block = g * GROUP + k
                grad = lax.dot_general(
                    cbuf[g, :, k * HBLK:(k + 1) * HBLK], a2[k // 2],
                    (((0,), (0,)), ((), ())), preferred_element_type=F32,
                )
                high, low = split(grad)
                turner = signed(block)
                turned = jnp.dot(turner, high, preferred_element_type=F32)
                turned = turned + jnp.dot(turner, low, preferred_element_type=F32)
                turned = turned * weight
                rot[block] = turned
                peaks.append(jnp.max(jnp.abs(turned), axis=0, keepdims=True))
            pk1[g] = jnp.concatenate(peaks + peaks, axis=0)
            for u in range(1, SIDE):
                put(pk1.at[g], rpx.at[g, u - 1], s_pk.at[g, 0], r_px.at[g], at_x(u))

        def peaks_over_y(g):
            wait_for(rpx.at[g], r_px.at[g])
            pk2[g] = jnp.maximum(
                jnp.maximum(pk1[g], rpx[g, 0]), jnp.maximum(rpx[g, 1], rpx[g, 2])
            )
            for u in range(1, SIDE):
                put(pk2.at[g], rpy.at[g, u - 1], s_pk.at[g, 1], r_py.at[g], at_y(u))

        def encode(g, t, c):
            block = g * GROUP + 2 * t + c
            scale = scl[pl.ds(2 * t + c, 1), :]
            up = jnp.broadcast_to(7.5 / scale, (8, scale.shape[1]))
            down = jnp.broadcast_to(scale * (1.0 / (15.0 * math.pi)), up.shape)
            rows = rowterm[t]

            def piece(n, carry):
                at = pl.multiple_of(n * 8, 8)
                value = rot[block, pl.ds(at, 8), :]
                col = colterm[pl.ds(pl.multiple_of(block * HBLK + n * 8, 8), 8), :]
                turns = value * up + (rows + jnp.concatenate([col] * 4, axis=1))
                part = turns - jnp.round(turns)
                square = part * part
                poly = SINE[5] * square + SINE[4]
                for k in (3, 2, 1, 0):
                    poly = poly * square + SINE[k]
                rot[block, pl.ds(at, 8), :] = value + down * (part * poly)
                return carry

            lax.fori_loop(0, HBLK // 8, piece, 0, unroll=4)

        def encode_group(g):
            wait_for(rpy.at[g], r_py.at[g])
            scl[...] = jnp.maximum(
                jnp.maximum(pk2[g], rpy[g, 0]), jnp.maximum(rpy[g, 1], rpy[g, 2])
            ) + 1e-06
            for t in range(2):
                encode(g, t, other)
                put(
                    rot.at[g * GROUP + 2 * t + other], rcore.at[g, t],
                    s_core.at[g, t], r_core.at[g, t], sibling,
                )
            for t in range(2):
                encode(g, t, core)

        half = HBLK // 2

        def lanes(t, u):
            here = x if t == 0 else y
            return pl.ds(pl.multiple_of(lax.rem(here + u, SIDE) * 128, 128), 128)

        top, bottom = pl.ds(0, half), pl.ds(half, half)

        def first_ring(g):
            for t in range(2):
                block = g * GROUP + 2 * t + core
                wait_for(rcore.at[g, t], r_core.at[g, t])
                for n in range(HBLK // 64):
                    rot[block, n * 64:(n + 1) * 64, :] += rcore[g, t, n * 64:(n + 1) * 64, :]
                mine, send = rot.at[block], s_one.at[g, t, 0]
                put(mine.at[top, lanes(t, 2)], ra.at[g, t, 0], send, r_a.at[g, t, 0], along(t, 1))
                put(mine.at[bottom, lanes(t, 2)], ra.at[g, t, 1], send, r_a.at[g, t, 1], along(t, 3))
                put(mine.at[bottom, lanes(t, 1)], rb.at[g, t, 0, bottom], send, r_b.at[g, t, 0], along(t, 1))
                put(mine.at[top, lanes(t, 3)], rb.at[g, t, 1, top], send, r_b.at[g, t, 1], along(t, 3))

        def first_ring_on(g):
            for t in range(2):
                block = g * GROUP + 2 * t + core
                mine, send = rot.at[block], s_one.at[g, t, 1]
                wait_for(ra.at[g, t, 0], r_a.at[g, t, 0])
                rot[block, top, lanes(t, 1)] += ra[g, t, 0]
                put(mine.at[top, lanes(t, 1)], rb.at[g, t, 0, top], send, r_b.at[g, t, 0], along(t, 1))
                wait_for(ra.at[g, t, 1], r_a.at[g, t, 1])
                rot[block, bottom, lanes(t, 3)] += ra[g, t, 1]
                put(mine.at[bottom, lanes(t, 3)], rb.at[g, t, 1, bottom], send, r_b.at[g, t, 1], along(t, 3))

        def rows_of(t, u, part):
            here = y if t == 0 else x
            return pl.ds(pl.multiple_of(lax.rem(here + u, SIDE) * 32 + part * 16, 16), 16)

        def second_ring(g):
            for t in range(2):
                block = g * GROUP + 2 * t + core
                wait_for(rb.at[g, t, 0], r_b.at[g, t, 0])
                wait_for(rb.at[g, t, 1], r_b.at[g, t, 1])
                summed = rot[block, :, lanes(t, 0)] + (rb[g, t, 0] + rb[g, t, 1])
                high, low = split(summed)
                turner = signed(block)
                contract = (((0,), (0,)), ((), ()))
                back = lax.dot_general(high, turner, contract, preferred_element_type=F32)
                back = back + lax.dot_general(low, turner, contract, preferred_element_type=F32)
                stage2[g, t] = back
                mine, send = stage2.at[g, t], s_two.at[g, t, 0]
                put(mine.at[rows_of(t, 2, 0)], ra2.at[g, t, 0], send, r_a2.at[g, t, 0], along(1 - t, 1))
                put(mine.at[rows_of(t, 2, 1)], ra2.at[g, t, 1], send, r_a2.at[g, t, 1], along(1 - t, 3))
                put(mine.at[rows_of(t, 1, 1)], rb2.at[g, t, 0, pl.ds(16, 16)], send, r_b2.at[g, t, 0], along(1 - t, 1))
                put(mine.at[rows_of(t, 3, 0)], rb2.at[g, t, 1, pl.ds(0, 16)], send, r_b2.at[g, t, 1], along(1 - t, 3))

        def second_ring_on(g):
            for t in range(2):
                mine, send = stage2.at[g, t], s_two.at[g, t, 1]
                wait_for(ra2.at[g, t, 0], r_a2.at[g, t, 0])
                stage2[g, t, rows_of(t, 1, 0), :] += ra2[g, t, 0]
                put(mine.at[rows_of(t, 1, 0)], rb2.at[g, t, 0, pl.ds(0, 16)], send, r_b2.at[g, t, 0], along(1 - t, 1))
                wait_for(ra2.at[g, t, 1], r_a2.at[g, t, 1])
                stage2[g, t, rows_of(t, 3, 1), :] += ra2[g, t, 1]
                put(mine.at[rows_of(t, 3, 1)], rb2.at[g, t, 1, pl.ds(16, 16)], send, r_b2.at[g, t, 1], along(1 - t, 3))

        def scatter_z(g):
            for t in range(2):
                wait_for(rb2.at[g, t, 0], r_b2.at[g, t, 0])
                wait_for(rb2.at[g, t, 1], r_b2.at[g, t, 1])
                for part in range(2):
                    summed = stage2[g, t, rows_of(t, 0, part), :] + (
                        rb2[g, t, 0, part * 16:(part + 1) * 16, :]
                        + rb2[g, t, 1, part * 16:(part + 1) * 16, :]
                    )
                    shares[g, 4 * t + 2 * part] = summed[:8]
                    shares[g, 4 * t + 2 * part + 1] = summed[8:]
            for u in range(1, depth):
                put(
                    shares.at[g, lax.rem(z + u, depth)], rz.at[g, u - 1],
                    s_z.at[g], r_z.at[g], at_z(u, core),
                )

        factor = 1.0 / (math.sqrt(HBLK) * math.sqrt(SIDE * SIDE * CORES * depth))

        def gather_z(g):
            wait_for(rz.at[g], r_z.at[g])
            total = shares[g, z]
            for u in range(depth - 1):
                total = total + rz[g, u]
            place = core * depth + z
            gathered[g, place] = total * factor
            for u in range(depth):
                for c in (core, other):
                    if u or c is other:
                        put(
                            gathered.at[g, place], gathered.at[g, place],
                            s_out.at[g], r_out.at[g], at_z(u, c),
                        )

        def deliver(g):
            wait_for(gathered.at[g, pl.ds(0, CORES * depth - 1)], r_out.at[g])
            for k in range(GROUP):
                at = pl.ds(pl.multiple_of((g * GROUP + k) * HBLK, HBLK), HBLK)
                for n in range(4):
                    out[8 * n:8 * n + 8, at] = gathered[g, (k % 2) * depth + 4 * (k // 2) + n]

        def settle(g):
            wait_for(rpx.at[g], s_pk.at[g, 0])
            wait_for(rpy.at[g], s_pk.at[g, 1])
            for t in range(2):
                wait_for(rcore.at[g, t], s_core.at[g, t])
                wait_for(rb.at[g, t], s_one.at[g, t, 0])
                wait_for(ra.at[g, t], s_one.at[g, t, 1])
                wait_for(rb2.at[g, t], s_two.at[g, t, 0])
                wait_for(ra2.at[g, t], s_two.at[g, t, 1])
            wait_for(rz.at[g], s_z.at[g])
            wait_for(gathered.at[g, pl.ds(0, CORES * depth - 1)], s_out.at[g])

        pl.semaphore_wait(barrier, len(peers))

        stages = [
            rotate, peaks_over_y, encode_group, first_ring, first_ring_on,
            second_ring, second_ring_on, scatter_z, gather_z, deliver,
        ]

        def step(s, carry):
            for late in reversed(range(len(stages))):
                g = s - late

                @pl.when((g >= 0) & (g < groups))
                def _(stage=stages[late], g=g):
                    stage(g)

            return carry

        lax.fori_loop(0, groups + len(stages) - 1, step, 0)

        def finish(g, carry):
            settle(g)
            return carry

        lax.fori_loop(0, groups, finish, 0)

    return kernel


def synchronize(depth, counts, dither_rows, dither_cols, signs, activations, cotangent):
    tokens, hidden = activations.shape
    cols = cotangent.shape[1]
    groups = cols // (GROUP * HBLK)
    blocks = groups * GROUP
    dma = pltpu.SemaphoreType.DMA
    vmem = pltpu.VMEM
    share = hidden // (SIDE * SIDE)
    flops = 2 * tokens * hidden * cols + 4 * hidden * cols * HBLK
    return pl.pallas_call(
        make_kernel(depth, groups),
        out_shape=jax.ShapeDtypeStruct((share, cols), F32),
        in_specs=[
            pl.BlockSpec(memory_space=pltpu.SMEM),
            pl.BlockSpec(memory_space=pltpu.VMEM),
            pl.BlockSpec(memory_space=pltpu.VMEM),
            pl.BlockSpec(memory_space=pltpu.VMEM),
            pl.BlockSpec(memory_space=pl.ANY),
            pl.BlockSpec(memory_space=pl.ANY),
        ],
        out_specs=pl.BlockSpec(memory_space=pltpu.VMEM),
        scratch_shapes=[
            vmem((groups, tokens, GROUP * HBLK), BF16),
            vmem((tokens, hidden), BF16),
            vmem((2, tokens, hidden), BF16),
            vmem((HBLK, HBLK), F32),
            vmem((cols, 128), F32),
            vmem((2, 8, hidden), F32),
            vmem((blocks, HBLK, hidden), F32),
            vmem((groups, 8, hidden), F32),
            vmem((groups, 8, hidden), F32),
            vmem((8, hidden), F32),
            vmem((groups, SIDE - 1, 8, hidden), F32),
            vmem((groups, SIDE - 1, 8, hidden), F32),
            vmem((groups, 2, HBLK, hidden), F32),
            vmem((groups, 2, 2, HBLK // 2, 128), F32),
            vmem((groups, 2, 2, HBLK, 128), F32),
            vmem((groups, 2, 2, 16, HBLK), F32),
            vmem((groups, 2, 2, 32, HBLK), F32),
            vmem((groups, 2, 128, HBLK), F32),
            vmem((groups, depth, 8, HBLK), F32),
            vmem((groups, depth - 1, 8, HBLK), F32),
            vmem((groups, CORES * depth, 8, HBLK), F32),
            dma((groups + 1,)),
            dma((groups, 2)),
            dma((groups,)),
            dma((groups,)),
            dma((groups, 2)),
            dma((groups, 2)),
            dma((groups, 2, 2)),
            dma((groups, 2, 2)),
            dma((groups, 2, 2)),
            dma((groups, 2, 2)),
            dma((groups, 2, 2)),
            dma((groups, 2, 2)),
            dma((groups,)),
            dma((groups,)),
            dma((groups,)),
            dma((groups,)),
        ],
        compiler_params=pltpu.CompilerParams(
            collective_id=0, has_side_effects=True, vmem_limit_bytes=56 * 2**20
        ),
        cost_estimate=pl.CostEstimate(
            flops=flops, bytes_accessed=2 * tokens * (hidden + cols), transcendentals=0
        ),
    )(counts, dither_rows, dither_cols, signs, activations, cotangent)


def solution(mesh):
    depth = mesh.shape["intra"] // CORES

    def body(activations, cotangent, counts, dither_rows, dither_cols, sign_bits):
        signs = (1 - 2 * sign_bits).astype(F32).reshape(-1, HBLK)
        return synchronize(
            depth, counts, dither_rows, dither_cols, signs, activations, cotangent
        )

    placed = (
        P(("inter", "intra"), None),
        P(("inter", "intra"), None),
        P("inter", "intra"),
        P("inter", None),
        P("inter", None),
        P(),
    )
    return jax.shard_map(
        body, mesh=mesh, in_specs=placed, out_specs=P("inter", None), check_vma=False
    )
```

```python
import math

import jax
import jax.numpy as jnp
from jax import lax
from jax.experimental import pallas as pl
from jax.experimental.pallas import tpu as pltpu
from jax.sharding import PartitionSpec as P

F32 = jnp.float32
BF16 = jnp.bfloat16
HBLK = 256
MB = 128
SIDE = 4
CORES = 2
GROUP = 4
LEAD = 32.78138732910156
SINE = tuple(c / LEAD for c in (
    6.283055782318115, -41.331214904785156, 81.36681365966797, -74.47799682617188,
))


def make_kernel(depth, groups):
    cols = groups * GROUP * HBLK

    def kernel(
        counts, drows, dcols, signs, a_hbm, c_hbm, out,
        cbuf, abuf, a2, hmat, colterm, rowterm, rot, pk1, pk2, scl,
        rplane, rpx, rpy, rcore, ra, rb, rb2, stage2, shares, rz, gathered,
        load_sem, s_pk, r_px, r_py, s_core, r_core, s_one, r_a, r_b,
        s_two, r_b2, s_z, r_z, s_out, r_out, s_pair, r_pair,
    ):
        i_me = lax.axis_index("inter")
        j_me = lax.axis_index("intra")
        x, y = i_me // SIDE, i_me % SIDE
        z, core = j_me // CORES, j_me % CORES
        other = 1 - core

        def at_x(u):
            return (lax.rem(x + u, SIDE) * SIDE + y, j_me)

        def at_y(u):
            return (x * SIDE + lax.rem(y + u, SIDE), j_me)

        def at_plane(u, v):
            return (lax.rem(x + u, SIDE) * SIDE + lax.rem(y + v, SIDE), j_me)

        def along(axis, u):
            to_x = lax.rem(x + u * (1 - axis), SIDE)
            to_y = lax.rem(y + u * axis, SIDE)
            return (to_x * SIDE + to_y, j_me)

        def at_z(u, c):
            return (i_me, lax.rem(z + u, depth) * CORES + c)

        sibling = at_z(0, other)

        def put(src, dst, send, recv, device):
            pltpu.make_async_remote_copy(
                src_ref=src, dst_ref=dst, send_sem=send, recv_sem=recv,
                device_id=device, device_id_type=pl.DeviceIdType.MESH,
            ).start()

        def wait_for(ref, sem):
            pltpu.make_async_copy(ref, ref, sem).wait()

        barrier = pltpu.get_barrier_semaphore()
        plane = [(u, v) for u in range(SIDE) for v in range(SIDE) if u or v]
        peers = [at_plane(u, v) for u, v in plane]
        peers += [at_z(u, core) for u in range(1, depth)] + [sibling]
        for device in peers:
            pl.semaphore_signal(
                barrier, inc=1, device_id=device, device_id_type=pl.DeviceIdType.MESH
            )

        load_a = pltpu.make_async_copy(a_hbm, abuf, load_sem.at[groups])
        load_a.start()
        width = GROUP * HBLK

        def load_c(g):
            return pltpu.make_async_copy(
                c_hbm.at[:, pl.ds(pl.multiple_of(g * width, width), width)],
                cbuf.at[g], load_sem.at[g],
            )

        for g in range(groups):
            load_c(g).start()

        first = lax.broadcasted_iota(jnp.int32, (HBLK, HBLK), 0)
        second = lax.broadcasted_iota(jnp.int32, (HBLK, HBLK), 1)
        both = first & second
        both = both ^ (both >> 4)
        both = both ^ (both >> 2)
        both = both ^ (both >> 1)
        hmat[...] = (1 - 2 * (both & 1)).astype(F32)

        load_a.wait()
        amount = counts[0, 0]
        hidden = abuf.shape[1]
        token = lax.broadcasted_iota(jnp.int32, abuf.shape, 0)
        a2[0] = jnp.where(token < amount * MB, abuf[...].astype(F32), 0.0).T.astype(BF16)
        sub = hidden // (SIDE * SIDE)
        for u in range(SIDE):
            for v in range(SIDE):
                a2[1, pl.ds((v * SIDE + u) * sub, sub), :] = a2[0, pl.ds((u * SIDE + v) * sub, sub), :]

        def dither_terms():
            def turn(tile, carry):
                at = pl.multiple_of(tile * 128, 128)
                row = dcols[:, pl.ds(at, 128)].astype(F32) * (1.0 / 256.0)
                colterm[pl.ds(at, 128), :] = jnp.broadcast_to(row, (128, 128)).T
                return carry

            lax.fori_loop(0, cols // 128, turn, 0, unroll=8)
            row_ints = jnp.broadcast_to(drows[...].astype(F32), (8, hidden))
            rowterm[0] = (row_ints + 0.5) * (1.0 / 256.0)
            to = lax.broadcasted_iota(jnp.int32, (hidden, hidden), 1)
            source = (to // sub % SIDE) * (SIDE * sub) + to // (SIDE * sub) * sub + to % sub
            fro = lax.broadcasted_iota(jnp.int32, (hidden, hidden), 0)
            order = jnp.where(fro == source, 1.0, 0.0).astype(BF16)
            row_ints = jnp.dot(row_ints.astype(BF16), order, preferred_element_type=F32)
            rowterm[1] = (row_ints + 0.5) * (1.0 / 256.0)

        counted = jnp.full((1, hidden), amount, jnp.int32)
        weight = jnp.where(counted == 1, 1.0 / math.sqrt(MB), 1.0 / math.sqrt(2 * MB))
        weight = jnp.where(counted == 3, 1.0 / math.sqrt(3 * MB), weight)
        weight = jnp.where(counted == 4, 1.0 / math.sqrt(4 * MB), weight)
        weight = weight * (1.0 / math.sqrt(HBLK))

        def signed(block):
            bits = signs[pl.ds(pl.multiple_of(block * HBLK, HBLK), HBLK)].reshape(1, HBLK)
            return (hmat[...] * (1 - 2 * bits).astype(F32)).astype(BF16)

        def split(value):
            high = value.astype(BF16)
            return high, (value - high.astype(F32)).astype(BF16)

        def rotate(g):
            load_c(g).wait()
            peaks = []
            for k in range(GROUP):
                block = g * GROUP + k
                grad = jnp.dot(
                    a2[k // 2], cbuf[g, :, k * HBLK:(k + 1) * HBLK], preferred_element_type=F32
                )
                high, low = split(grad)
                turner = signed(block)
                lasts = (((1,), (1,)), ((), ()))
                turned = lax.dot_general(turner, high, lasts, preferred_element_type=F32)
                turned = turned + lax.dot_general(turner, low, lasts, preferred_element_type=F32)
                turned = turned * weight
                rot[block] = turned
                peaks.append(jnp.max(jnp.abs(turned), axis=0, keepdims=True))
            pk1[g] = jnp.concatenate(peaks + peaks, axis=0)

            @pl.when(g == 0)
            def _():
                pl.semaphore_wait(barrier, len(peers))

            @pl.when(g == 0)
            def _():
                for k, (u, v) in enumerate(plane):
                    put(pk1.at[0], rplane.at[k], s_pk.at[0, 0], r_px.at[0], at_plane(u, v))

            @pl.when(g > 0)
            def _():
                for u in range(1, SIDE):
                    put(pk1.at[g], rpx.at[g, u - 1], s_pk.at[g, 0], r_px.at[g], at_x(u))

        def peaks_over_y(g):
            wait_for(rpx.at[g], r_px.at[g])
            pk2[g] = jnp.maximum(
                jnp.maximum(pk1[g], rpx[g, 0]), jnp.maximum(rpx[g, 1], rpx[g, 2])
            )
            for u in range(1, SIDE):
                put(pk2.at[g], rpy.at[g, u - 1], s_pk.at[g, 1], r_py.at[g], at_y(u))

        def encode(g, t, c):
            block = g * GROUP + 2 * t + c
            scale = scl[pl.ds(2 * t + c, 1), :]
            up = jnp.broadcast_to(7.5 / scale, (8, scale.shape[1]))
            down = jnp.broadcast_to(scale * (LEAD / (15.0 * math.pi)), up.shape)
            rows = rowterm[t]

            def piece(n, carry):
                at = pl.multiple_of(n * 8, 8)
                value = rot[block, pl.ds(at, 8), :]
                col = colterm[pl.ds(pl.multiple_of(block * HBLK + n * 8, 8), 8), :]
                turns = value * up + (rows + jnp.concatenate([col] * 4, axis=1))
                part = turns - jnp.round(turns)
                square = part * part
                poly = square + SINE[3]
                for k in (2, 1, 0):
                    poly = poly * square + SINE[k]
                rot[block, pl.ds(at, 8), :] = value + down * (part * poly)
                return carry

            lax.fori_loop(0, HBLK // 8, piece, 0, unroll=4)

        def scales(g):
            @pl.when(g == 0)
            def _():
                wait_for(rplane, r_px.at[0])
                top_peaks = pk1[0]
                for k in range(len(plane)):
                    top_peaks = jnp.maximum(top_peaks, rplane[k])
                scl[...] = top_peaks + 1e-06

            @pl.when(g > 0)
            def _():
                wait_for(rpy.at[g], r_py.at[g])
                scl[...] = jnp.maximum(
                    jnp.maximum(pk2[g], rpy[g, 0]), jnp.maximum(rpy[g, 1], rpy[g, 2])
                ) + 1e-06

        def encode_other(g, t):
            encode(g, t, other)
            put(
                rot.at[g * GROUP + 2 * t + other], rcore.at[g, t],
                s_core.at[g, t], r_core.at[g, t], sibling,
            )

        def encode_own(g, t):
            encode(g, t, core)

        half = HBLK // 2

        def lanes(t, u):
            here = x + t * (y - x)
            return pl.ds(pl.multiple_of(lax.rem(here + u, SIDE) * 128, 128), 128)

        top, bottom = pl.ds(0, half), pl.ds(half, half)

        def first_ring(g, t):
            block = g * GROUP + 2 * t + core
            wait_for(rcore.at[g, t], r_core.at[g, t])
            for n in range(HBLK // 64):
                rot[block, n * 64:(n + 1) * 64, :] += rcore[g, t, n * 64:(n + 1) * 64, :]
            mine, send = rot.at[block], s_one.at[g, t, 0]
            put(mine.at[top, lanes(t, 2)], ra.at[g, t, 0], send, r_a.at[g, t, 0], along(t, 1))
            put(mine.at[bottom, lanes(t, 2)], ra.at[g, t, 1], send, r_a.at[g, t, 1], along(t, 3))
            put(mine.at[bottom, lanes(t, 1)], rb.at[g, t, 0, bottom], send, r_b.at[g, t, 0], along(t, 1))
            put(mine.at[top, lanes(t, 3)], rb.at[g, t, 1, top], send, r_b.at[g, t, 1], along(t, 3))

        def first_ring_on(g, t):
            block = g * GROUP + 2 * t + core
            mine, send = rot.at[block], s_one.at[g, t, 1]
            wait_for(ra.at[g, t, 0], r_a.at[g, t, 0])
            rot[block, top, lanes(t, 1)] += ra[g, t, 0]
            put(mine.at[top, lanes(t, 1)], rb.at[g, t, 0, top], send, r_b.at[g, t, 0], along(t, 1))
            wait_for(ra.at[g, t, 1], r_a.at[g, t, 1])
            rot[block, bottom, lanes(t, 3)] += ra[g, t, 1]
            put(mine.at[bottom, lanes(t, 3)], rb.at[g, t, 1, bottom], send, r_b.at[g, t, 1], along(t, 3))

        def rows_of(t, u):
            here = y + t * (x - y)
            return pl.ds(pl.multiple_of(lax.rem(here + u, SIDE) * 32, 32), 32)

        def second_ring(g, t):
            block = g * GROUP + 2 * t + core
            wait_for(rb.at[g, t, 0], r_b.at[g, t, 0])
            wait_for(rb.at[g, t, 1], r_b.at[g, t, 1])
            summed = rot[block, :, lanes(t, 0)] + (rb[g, t, 0] + rb[g, t, 1])
            high, low = split(summed)
            turner = signed(block)
            contract = (((0,), (0,)), ((), ()))
            back = lax.dot_general(high, turner, contract, preferred_element_type=F32)
            back = back + lax.dot_general(low, turner, contract, preferred_element_type=F32)
            stage2[g, t] = back
            mine, send = stage2.at[g, t], s_two.at[g, t]
            for u in range(1, SIDE):
                put(mine.at[rows_of(t, u)], rb2.at[g, t, u - 1], send, r_b2.at[g, t], along(1 - t, u))

        def second_sum(g, t):
            wait_for(rb2.at[g, t], r_b2.at[g, t])
            summed = (stage2[g, t, rows_of(t, 0), :] + rb2[g, t, 0]) + (rb2[g, t, 1] + rb2[g, t, 2])
            for n in range(4):
                shares[g, 4 * t + n] = summed[8 * n:8 * n + 8]

        def scatter_z(g):
            for u in range(1, depth):
                put(
                    shares.at[g, lax.rem(z + u, depth)], rz.at[g, u - 1],
                    s_z.at[g], r_z.at[g], at_z(u, core),
                )

        def gather_z(g):
            wait_for(rz.at[g], r_z.at[g])
            total = shares[g, z]
            for u in range(depth - 1):
                total = total + rz[g, u]
            place = core * depth + z
            gathered[g, place] = total
            for u in range(1, depth):
                put(
                    gathered.at[g, place], gathered.at[g, place],
                    s_out.at[g], r_out.at[g], at_z(u, core),
                )

        def half_of(g, c):
            return gathered.at[g, pl.ds(c * depth, depth)]

        def share_core(g):
            wait_for(rz.at[g], r_out.at[g])
            put(half_of(g, core), half_of(g, core), s_pair.at[g], r_pair.at[g], sibling)

        def deliver(g):
            wait_for(half_of(g, other), r_pair.at[g])
            for k in range(GROUP):
                at = pl.ds(pl.multiple_of((g * GROUP + k) * HBLK, HBLK), HBLK)
                for n in range(4):
                    out[8 * n:8 * n + 8, at] = gathered[g, (k % 2) * depth + 4 * (k // 2) + n]

        def settle(g):
            @pl.when(g == 0)
            def _():
                wait_for(rplane, s_pk.at[0, 0])

            @pl.when(g > 0)
            def _():
                wait_for(rpx.at[g], s_pk.at[g, 0])
                wait_for(rpy.at[g], s_pk.at[g, 1])

            for t in range(2):
                wait_for(rcore.at[g, t], s_core.at[g, t])
                wait_for(rb.at[g, t], s_one.at[g, t, 0])
                wait_for(ra.at[g, t], s_one.at[g, t, 1])
                wait_for(rb2.at[g, t], s_two.at[g, t])
            wait_for(rz.at[g], s_z.at[g])
            wait_for(rz.at[g], s_out.at[g])
            wait_for(half_of(g, core), s_pair.at[g])

        def at_step(g, stage):
            @pl.when((g >= 0) & (g < groups))
            def _():
                stage(g)

        def at_half(h, stage):
            @pl.when((h >= 0) & (h < 2 * groups))
            def _():
                stage(h // 2, h % 2)

        def after_pair(h, stage):
            @pl.when((h >= 0) & (h < 2 * groups) & (h % 2 == 1))
            def _():
                stage(h // 2)

        def before_pair(h, stage):
            @pl.when((h >= 0) & (h < 2 * groups) & (h % 2 == 0))
            def _():
                stage(h // 2)

        ahead = 2

        def early(s, carry):
            rotate(s)

            @pl.when(s > ahead)
            def _():
                peaks_over_y(s - ahead)

            return carry

        lax.fori_loop(0, groups, early, 0)
        dither_terms()

        def late(s, carry):
            before_pair(s + 2 * (groups - ahead), peaks_over_y)
            before_pair(s, scales)
            at_half(s, encode_other)
            at_half(s, encode_own)
            at_half(s - 1, first_ring)
            at_half(s - 4, first_ring_on)
            at_half(s - 7, second_ring)
            at_half(s - 9, second_sum)
            after_pair(s - 9, scatter_z)
            after_pair(s - 12, gather_z)
            after_pair(s - 15, share_core)
            return carry

        lax.fori_loop(0, 2 * groups + 15, late, 0)

        def finish(g, carry):
            deliver(g)
            settle(g)
            return carry

        lax.fori_loop(0, groups, finish, 0)

    return kernel


def synchronize(depth, counts, dither_rows, dither_cols, signs, activations, cotangent):
    tokens, hidden = activations.shape
    cols = cotangent.shape[1]
    groups = cols // (GROUP * HBLK)
    blocks = groups * GROUP
    dma = pltpu.SemaphoreType.DMA
    vmem = pltpu.VMEM
    share = hidden // (SIDE * SIDE)
    flops = 2 * tokens * hidden * cols + 4 * hidden * cols * HBLK
    return pl.pallas_call(
        make_kernel(depth, groups),
        out_shape=jax.ShapeDtypeStruct((share, cols), F32),
        in_specs=[
            pl.BlockSpec(memory_space=pltpu.SMEM),
            pl.BlockSpec(memory_space=pltpu.VMEM),
            pl.BlockSpec(memory_space=pltpu.VMEM),
            pl.BlockSpec(memory_space=pltpu.VMEM),
            pl.BlockSpec(memory_space=pl.ANY),
            pl.BlockSpec(memory_space=pl.ANY),
        ],
        out_specs=pl.BlockSpec(memory_space=pltpu.VMEM),
        scratch_shapes=[
            vmem((groups, tokens, GROUP * HBLK), BF16),
            vmem((tokens, hidden), BF16),
            vmem((2, hidden, tokens), BF16),
            vmem((HBLK, HBLK), F32),
            vmem((cols, 128), F32),
            vmem((2, 8, hidden), F32),
            vmem((blocks, HBLK, hidden), F32),
            vmem((groups, 8, hidden), F32),
            vmem((groups, 8, hidden), F32),
            vmem((8, hidden), F32),
            vmem((SIDE * SIDE - 1, 8, hidden), F32),
            vmem((groups, SIDE - 1, 8, hidden), F32),
            vmem((groups, SIDE - 1, 8, hidden), F32),
            vmem((groups, 2, HBLK, hidden), F32),
            vmem((groups, 2, 2, HBLK // 2, 128), F32),
            vmem((groups, 2, 2, HBLK, 128), F32),
            vmem((groups, 2, SIDE - 1, 32, HBLK), F32),
            vmem((groups, 2, 128, HBLK), F32),
            vmem((groups, depth, 8, HBLK), F32),
            vmem((groups, depth - 1, 8, HBLK), F32),
            vmem((groups, CORES * depth, 8, HBLK), F32),
            dma((groups + 1,)),
            dma((groups, 2)),
            dma((groups,)),
            dma((groups,)),
            dma((groups, 2)),
            dma((groups, 2)),
            dma((groups, 2, 2)),
            dma((groups, 2, 2)),
            dma((groups, 2, 2)),
            dma((groups, 2)),
            dma((groups, 2)),
            dma((groups,)),
            dma((groups,)),
            dma((groups,)),
            dma((groups,)),
            dma((groups,)),
            dma((groups,)),
        ],
        compiler_params=pltpu.CompilerParams(
            collective_id=0, has_side_effects=True, vmem_limit_bytes=56 * 2**20
        ),
        cost_estimate=pl.CostEstimate(
            flops=flops, bytes_accessed=2 * tokens * (hidden + cols), transcendentals=0
        ),
    )(counts, dither_rows, dither_cols, signs, activations, cotangent)


def solution(mesh):
    depth = mesh.shape["intra"] // CORES

    def body(activations, cotangent, counts, dither_rows, dither_cols, sign_bits):
        summed = synchronize(
            depth, counts, dither_rows, dither_cols, sign_bits, activations, cotangent
        )
        return summed * (1.0 / (math.sqrt(HBLK) * math.sqrt(mesh.size)))

    placed = (
        P(("inter", "intra"), None),
        P(("inter", "intra"), None),
        P("inter", "intra"),
        P("inter", None),
        P("inter", None),
        P(),
    )
    return jax.shard_map(
        body, mesh=mesh, in_specs=placed, out_specs=P("inter", None), check_vma=False
    )
```

```python
import math

import jax
import jax.numpy as jnp
from jax import lax
from jax.experimental import pallas as pl
from jax.experimental.pallas import tpu as pltpu
from jax.sharding import PartitionSpec as P

F32 = jnp.float32
BF16 = jnp.bfloat16
HBLK = 256
MB = 128
SIDE = 4
CORES = 2
GROUP = 4
LEAD = 32.78138732910156
SINE = tuple(c / LEAD for c in (
    6.283055782318115, -41.331214904785156, 81.36681365966797, -74.47799682617188,
))


def make_kernel(depth, groups):
    cols = groups * GROUP * HBLK

    def kernel(
        counts, drows_hbm, dcols_hbm, signs_hbm, a_hbm, c_hbm, out_hbm,
        drows, dcols, signs, out,
        cbuf, abuf, a2, hmat, colterm, rowterm, rot, pk1, pk2, scl,
        rplane, rpx, rpy, rcore, ra, rb, rb2, stage2, shares, rz, gathered,
        load_sem, store_sem, s_pk, r_px, r_py, s_core, r_core, s_one, r_a, r_b,
        s_two, r_b2, s_z, r_z, s_out, r_out, s_pair, r_pair,
    ):
        i_me = lax.axis_index("inter")
        j_me = lax.axis_index("intra")
        x, y = i_me // SIDE, i_me % SIDE
        z, core = j_me // CORES, j_me % CORES
        other = 1 - core

        def at_x(u):
            return (lax.rem(x + u, SIDE) * SIDE + y, j_me)

        def at_y(u):
            return (x * SIDE + lax.rem(y + u, SIDE), j_me)

        def at_plane(u, v):
            return (lax.rem(x + u, SIDE) * SIDE + lax.rem(y + v, SIDE), j_me)

        def along(axis, u):
            to_x = lax.rem(x + u * (1 - axis), SIDE)
            to_y = lax.rem(y + u * axis, SIDE)
            return (to_x * SIDE + to_y, j_me)

        def at_z(u, c):
            return (i_me, lax.rem(z + u, depth) * CORES + c)

        sibling = at_z(0, other)

        def put(src, dst, send, recv, device):
            pltpu.make_async_remote_copy(
                src_ref=src, dst_ref=dst, send_sem=send, recv_sem=recv,
                device_id=device, device_id_type=pl.DeviceIdType.MESH,
            ).start()

        def wait_for(ref, sem):
            pltpu.make_async_copy(ref, ref, sem).wait()

        barrier = pltpu.get_barrier_semaphore()
        plane = [(u, v) for u in range(SIDE) for v in range(SIDE) if u or v]
        peers = [at_plane(u, v) for u, v in plane]
        peers += [at_z(u, core) for u in range(1, depth)] + [sibling]
        for device in peers:
            pl.semaphore_signal(
                barrier, inc=1, device_id=device, device_id_type=pl.DeviceIdType.MESH
            )

        load_a = pltpu.make_async_copy(a_hbm, abuf, load_sem.at[groups])
        load_a.start()
        load_signs = pltpu.make_async_copy(signs_hbm, signs, load_sem.at[groups + 1])
        load_rows = pltpu.make_async_copy(drows_hbm, drows, load_sem.at[groups + 2])
        load_cols = pltpu.make_async_copy(dcols_hbm, dcols, load_sem.at[groups + 3])
        load_signs.start()
        width = GROUP * HBLK

        def load_c(g):
            return pltpu.make_async_copy(
                c_hbm.at[:, pl.ds(pl.multiple_of(g * width, width), width)],
                cbuf.at[g], load_sem.at[g],
            )

        for g in range(groups):
            load_c(g).start()
        load_rows.start()
        load_cols.start()

        first = lax.broadcasted_iota(jnp.int32, (HBLK, HBLK), 0)
        second = lax.broadcasted_iota(jnp.int32, (HBLK, HBLK), 1)
        both = first & second
        both = both ^ (both >> 4)
        both = both ^ (both >> 2)
        both = both ^ (both >> 1)
        hmat[...] = (1 - 2 * (both & 1)).astype(F32)

        load_a.wait()
        amount = counts[0, 0]
        hidden = abuf.shape[1]
        token = lax.broadcasted_iota(jnp.int32, abuf.shape, 0)
        a2[0] = jnp.where(token < amount * MB, abuf[...].astype(F32), 0.0).T.astype(BF16)
        sub = hidden // (SIDE * SIDE)
        for u in range(SIDE):
            for v in range(SIDE):
                a2[1, pl.ds((v * SIDE + u) * sub, sub), :] = a2[0, pl.ds((u * SIDE + v) * sub, sub), :]

        def dither_terms():
            def turn(tile, carry):
                at = pl.multiple_of(tile * 128, 128)
                row = dcols[:, pl.ds(at, 128)].astype(F32) * (1.0 / 256.0)
                colterm[pl.ds(at, 128), :] = jnp.broadcast_to(row, (128, 128)).T
                return carry

            lax.fori_loop(0, cols // 128, turn, 0, unroll=8)
            row_ints = jnp.broadcast_to(drows[...].astype(F32), (8, hidden))
            rowterm[0] = (row_ints + 0.5) * (1.0 / 256.0)
            to = lax.broadcasted_iota(jnp.int32, (hidden, hidden), 1)
            source = (to // sub % SIDE) * (SIDE * sub) + to // (SIDE * sub) * sub + to % sub
            fro = lax.broadcasted_iota(jnp.int32, (hidden, hidden), 0)
            order = jnp.where(fro == source, 1.0, 0.0).astype(BF16)
            row_ints = jnp.dot(row_ints.astype(BF16), order, preferred_element_type=F32)
            rowterm[1] = (row_ints + 0.5) * (1.0 / 256.0)

        counted = jnp.full((1, hidden), amount, jnp.int32)
        weight = jnp.where(counted == 1, 1.0 / math.sqrt(MB), 1.0 / math.sqrt(2 * MB))
        weight = jnp.where(counted == 3, 1.0 / math.sqrt(3 * MB), weight)
        weight = jnp.where(counted == 4, 1.0 / math.sqrt(4 * MB), weight)
        weight = weight * (1.0 / math.sqrt(HBLK))

        def signed(block):
            bits = signs[pl.ds(pl.multiple_of(block * HBLK, HBLK), HBLK)].reshape(1, HBLK)
            return (hmat[...] * (1 - 2 * bits).astype(F32)).astype(BF16)

        def split(value):
            high = value.astype(BF16)
            return high, (value - high.astype(F32)).astype(BF16)

        wide = pk1.shape[2]

        def rotate(g):
            load_c(g).wait()
            peaks = []
            for k in range(GROUP):
                block = g * GROUP + k
                grad = jnp.dot(
                    a2[k // 2], cbuf[g, :, k * HBLK:(k + 1) * HBLK], preferred_element_type=F32
                )
                high, low = split(grad)
                turner = signed(block)
                lasts = (((1,), (1,)), ((), ()))
                turned = lax.dot_general(turner, high, lasts, preferred_element_type=F32)
                turned = turned + lax.dot_general(turner, low, lasts, preferred_element_type=F32)
                turned = turned * weight
                rot[block] = turned
                peaks.append(jnp.max(jnp.abs(turned), axis=0, keepdims=True))
            pk1[g] = jnp.concatenate(
                [p[:, :wide] for p in peaks] + [p[:, wide:] for p in peaks], axis=0
            )

            @pl.when(g == 0)
            def _():
                pl.semaphore_wait(barrier, len(peers))

            @pl.when(g == 0)
            def _():
                for k, (u, v) in enumerate(plane):
                    put(pk1.at[0], rplane.at[k], s_pk.at[0, 0], r_px.at[0], at_plane(u, v))

            @pl.when(g > 0)
            def _():
                for u in range(1, SIDE):
                    put(pk1.at[g], rpx.at[g, u - 1], s_pk.at[g, 0], r_px.at[g], at_x(u))

        def peaks_over_y(g):
            wait_for(rpx.at[g], r_px.at[g])
            pk2[g] = jnp.maximum(
                jnp.maximum(pk1[g], rpx[g, 0]), jnp.maximum(rpx[g, 1], rpx[g, 2])
            )
            for u in range(1, SIDE):
                put(pk2.at[g], rpy.at[g, u - 1], s_pk.at[g, 1], r_py.at[g], at_y(u))

        def encode(g, t, c):
            block = g * GROUP + 2 * t + c
            scale = scl[pl.ds(2 * t + c, 1), :]
            up = jnp.broadcast_to(7.5 / scale, (8, scale.shape[1]))
            down = jnp.broadcast_to(scale * (LEAD / (15.0 * math.pi)), up.shape)
            rows = rowterm[t]

            def piece(n, carry):
                at = pl.multiple_of(n * 8, 8)
                value = rot[block, pl.ds(at, 8), :]
                col = colterm[pl.ds(pl.multiple_of(block * HBLK + n * 8, 8), 8), :]
                turns = value * up + (rows + jnp.concatenate([col] * 4, axis=1))
                part = turns - jnp.round(turns)
                square = part * part
                poly = square + SINE[3]
                for k in (2, 1, 0):
                    poly = poly * square + SINE[k]
                rot[block, pl.ds(at, 8), :] = value + down * (part * poly)
                return carry

            lax.fori_loop(0, HBLK // 8, piece, 0, unroll=4)

        def keep(found):
            scl[:, :wide] = found[:GROUP] + 1e-06
            scl[:, wide:] = found[GROUP:] + 1e-06

        def scales(g):
            @pl.when(g == 0)
            def _():
                wait_for(rplane, r_px.at[0])
                top_peaks = pk1[0]
                for k in range(len(plane)):
                    top_peaks = jnp.maximum(top_peaks, rplane[k])
                keep(top_peaks)

            @pl.when(g > 0)
            def _():
                wait_for(rpy.at[g], r_py.at[g])
                keep(jnp.maximum(
                    jnp.maximum(pk2[g], rpy[g, 0]), jnp.maximum(rpy[g, 1], rpy[g, 2])
                ))

        def encode_other(g, t):
            encode(g, t, other)
            put(
                rot.at[g * GROUP + 2 * t + other], rcore.at[g, t],
                s_core.at[g, t], r_core.at[g, t], sibling,
            )

        def encode_own(g, t):
            encode(g, t, core)

        half = HBLK // 2

        def lanes(t, u):
            here = x + t * (y - x)
            return pl.ds(pl.multiple_of(lax.rem(here + u, SIDE) * 128, 128), 128)

        top, bottom = pl.ds(0, half), pl.ds(half, half)

        def first_ring(g, t):
            block = g * GROUP + 2 * t + core
            wait_for(rcore.at[g, t], r_core.at[g, t])
            for n in range(HBLK // 64):
                rot[block, n * 64:(n + 1) * 64, :] += rcore[g, t, n * 64:(n + 1) * 64, :]
            mine, send = rot.at[block], s_one.at[g, t, 0]
            put(mine.at[top, lanes(t, 2)], ra.at[g, t, 0], send, r_a.at[g, t, 0], along(t, 1))
            put(mine.at[bottom, lanes(t, 2)], ra.at[g, t, 1], send, r_a.at[g, t, 1], along(t, 3))
            put(mine.at[bottom, lanes(t, 1)], rb.at[g, t, 0, bottom], send, r_b.at[g, t, 0], along(t, 1))
            put(mine.at[top, lanes(t, 3)], rb.at[g, t, 1, top], send, r_b.at[g, t, 1], along(t, 3))

        def first_ring_on(g, t):
            block = g * GROUP + 2 * t + core
            mine, send = rot.at[block], s_one.at[g, t, 1]
            wait_for(ra.at[g, t, 0], r_a.at[g, t, 0])
            rot[block, top, lanes(t, 1)] += ra[g, t, 0]
            put(mine.at[top, lanes(t, 1)], rb.at[g, t, 0, top], send, r_b.at[g, t, 0], along(t, 1))
            wait_for(ra.at[g, t, 1], r_a.at[g, t, 1])
            rot[block, bottom, lanes(t, 3)] += ra[g, t, 1]
            put(mine.at[bottom, lanes(t, 3)], rb.at[g, t, 1, bottom], send, r_b.at[g, t, 1], along(t, 3))

        def rows_of(t, u):
            here = y + t * (x - y)
            return pl.ds(pl.multiple_of(lax.rem(here + u, SIDE) * 32, 32), 32)

        def second_ring(g, t):
            block = g * GROUP + 2 * t + core
            wait_for(rb.at[g, t, 0], r_b.at[g, t, 0])
            wait_for(rb.at[g, t, 1], r_b.at[g, t, 1])
            summed = rot[block, :, lanes(t, 0)] + (rb[g, t, 0] + rb[g, t, 1])
            high, low = split(summed)
            turner = signed(block)
            contract = (((0,), (0,)), ((), ()))
            back = lax.dot_general(high, turner, contract, preferred_element_type=F32)
            back = back + lax.dot_general(low, turner, contract, preferred_element_type=F32)
            stage2[g, t] = back
            mine, send = stage2.at[g, t], s_two.at[g, t]
            for u in range(1, SIDE):
                put(mine.at[rows_of(t, u)], rb2.at[g, t, u - 1], send, r_b2.at[g, t], along(1 - t, u))

        def second_sum(g, t):
            wait_for(rb2.at[g, t], r_b2.at[g, t])
            summed = (stage2[g, t, rows_of(t, 0), :] + rb2[g, t, 0]) + (rb2[g, t, 1] + rb2[g, t, 2])
            for n in range(4):
                shares[g, 4 * t + n] = summed[8 * n:8 * n + 8]

        def scatter_z(g):
            for u in range(1, depth):
                put(
                    shares.at[g, lax.rem(z + u, depth)], rz.at[g, u - 1],
                    s_z.at[g], r_z.at[g], at_z(u, core),
                )

        def gather_z(g):
            wait_for(rz.at[g], r_z.at[g])
            total = shares[g, z]
            for u in range(depth - 1):
                total = total + rz[g, u]
            place = core * depth + z
            gathered[g, place] = total
            for u in range(1, depth):
                put(
                    gathered.at[g, place], gathered.at[g, place],
                    s_out.at[g], r_out.at[g], at_z(u, core),
                )

        def half_of(g, c):
            return gathered.at[g, pl.ds(c * depth, depth)]

        def share_core(g):
            wait_for(rz.at[g], r_out.at[g])
            put(half_of(g, core), half_of(g, core), s_pair.at[g], r_pair.at[g], sibling)

        def store(g):
            at = pl.ds(pl.multiple_of(g * width, width), width)
            return pltpu.make_async_copy(out.at[:, at], out_hbm.at[:, at], store_sem.at[g])

        def deliver(g):
            wait_for(half_of(g, other), r_pair.at[g])
            for k in range(GROUP):
                at = pl.ds(pl.multiple_of((g * GROUP + k) * HBLK, HBLK), HBLK)
                for n in range(4):
                    out[8 * n:8 * n + 8, at] = gathered[g, (k % 2) * depth + 4 * (k // 2) + n]
            store(g).start()

        def settle(g):
            @pl.when(g == 0)
            def _():
                wait_for(rplane, s_pk.at[0, 0])

            @pl.when(g > 0)
            def _():
                wait_for(rpx.at[g], s_pk.at[g, 0])
                wait_for(rpy.at[g], s_pk.at[g, 1])

            for t in range(2):
                wait_for(rcore.at[g, t], s_core.at[g, t])
                wait_for(rb.at[g, t], s_one.at[g, t, 0])
                wait_for(ra.at[g, t], s_one.at[g, t, 1])
                wait_for(rb2.at[g, t], s_two.at[g, t])
            wait_for(rz.at[g], s_z.at[g])
            wait_for(rz.at[g], s_out.at[g])
            wait_for(half_of(g, core), s_pair.at[g])

        def at_step(g, stage):
            @pl.when((g >= 0) & (g < groups))
            def _():
                stage(g)

        def at_half(h, stage):
            @pl.when((h >= 0) & (h < 2 * groups))
            def _():
                stage(h // 2, h % 2)

        def after_pair(h, stage):
            @pl.when((h >= 0) & (h < 2 * groups) & (h % 2 == 1))
            def _():
                stage(h // 2)

        def before_pair(h, stage):
            @pl.when((h >= 0) & (h < 2 * groups) & (h % 2 == 0))
            def _():
                stage(h // 2)

        ahead = 2

        def early(s, carry):
            rotate(s)

            @pl.when(s > ahead)
            def _():
                peaks_over_y(s - ahead)

            return carry

        load_signs.wait()
        lax.fori_loop(0, groups, early, 0)
        load_rows.wait()
        load_cols.wait()
        dither_terms()

        def late(s, carry):
            before_pair(s + 2 * (groups - ahead), peaks_over_y)
            before_pair(s, scales)
            at_half(s, encode_other)
            at_half(s - 1, first_ring)
            at_half(s, encode_own)
            at_half(s - 4, first_ring_on)
            at_half(s - 7, second_ring)
            at_half(s - 9, second_sum)
            after_pair(s - 9, scatter_z)
            after_pair(s - 12, gather_z)
            after_pair(s - 15, share_core)
            return carry

        lax.fori_loop(0, 2 * groups + 15, late, 0)

        def hand_out(g, carry):
            deliver(g)
            return carry

        lax.fori_loop(0, groups, hand_out, 0)

        def finish(g, carry):
            settle(g)
            store(g).wait()
            return carry

        lax.fori_loop(0, groups, finish, 0)

    return kernel


def synchronize(depth, counts, dither_rows, dither_cols, signs, activations, cotangent):
    tokens, hidden = activations.shape
    cols = cotangent.shape[1]
    groups = cols // (GROUP * HBLK)
    blocks = groups * GROUP
    dma = pltpu.SemaphoreType.DMA
    vmem = pltpu.VMEM
    share = hidden // (SIDE * SIDE)
    flops = 2 * tokens * hidden * cols + 4 * hidden * cols * HBLK
    return pl.pallas_call(
        make_kernel(depth, groups),
        out_shape=jax.ShapeDtypeStruct((share, cols), F32),
        in_specs=[
            pl.BlockSpec(memory_space=pltpu.SMEM),
            pl.BlockSpec(memory_space=pl.ANY),
            pl.BlockSpec(memory_space=pl.ANY),
            pl.BlockSpec(memory_space=pl.ANY),
            pl.BlockSpec(memory_space=pl.ANY),
            pl.BlockSpec(memory_space=pl.ANY),
        ],
        out_specs=pl.BlockSpec(memory_space=pl.ANY),
        scratch_shapes=[
            vmem((1, hidden), jnp.int32),
            vmem((1, cols), jnp.int32),
            vmem((cols,), jnp.int32),
            vmem((share, cols), F32),
            vmem((groups, tokens, GROUP * HBLK), BF16),
            vmem((tokens, hidden), BF16),
            vmem((2, hidden, tokens), BF16),
            vmem((HBLK, HBLK), F32),
            vmem((cols, 128), F32),
            vmem((2, 8, hidden), F32),
            vmem((blocks, HBLK, hidden), F32),
            vmem((groups, 8, hidden // 2), F32),
            vmem((groups, 8, hidden // 2), F32),
            vmem((GROUP, hidden), F32),
            vmem((SIDE * SIDE - 1, 8, hidden // 2), F32),
            vmem((groups, SIDE - 1, 8, hidden // 2), F32),
            vmem((groups, SIDE - 1, 8, hidden // 2), F32),
            vmem((groups, 2, HBLK, hidden), F32),
            vmem((groups, 2, 2, HBLK // 2, 128), F32),
            vmem((groups, 2, 2, HBLK, 128), F32),
            vmem((groups, 2, SIDE - 1, 32, HBLK), F32),
            vmem((groups, 2, 128, HBLK), F32),
            vmem((groups, depth, 8, HBLK), F32),
            vmem((groups, depth - 1, 8, HBLK), F32),
            vmem((groups, CORES * depth, 8, HBLK), F32),
            dma((groups + 4,)),
            dma((groups,)),
            dma((groups, 2)),
            dma((groups,)),
            dma((groups,)),
            dma((groups, 2)),
            dma((groups, 2)),
            dma((groups, 2, 2)),
            dma((groups, 2, 2)),
            dma((groups, 2, 2)),
            dma((groups, 2)),
            dma((groups, 2)),
            dma((groups,)),
            dma((groups,)),
            dma((groups,)),
            dma((groups,)),
            dma((groups,)),
            dma((groups,)),
        ],
        compiler_params=pltpu.CompilerParams(
            collective_id=0, has_side_effects=True, vmem_limit_bytes=56 * 2**20
        ),
        cost_estimate=pl.CostEstimate(
            flops=flops, bytes_accessed=2 * tokens * (hidden + cols), transcendentals=0
        ),
    )(counts, dither_rows, dither_cols, signs, activations, cotangent)


def solution(mesh):
    depth = mesh.shape["intra"] // CORES

    def body(activations, cotangent, counts, dither_rows, dither_cols, sign_bits):
        summed = synchronize(
            depth, counts, dither_rows, dither_cols, sign_bits, activations, cotangent
        )
        return summed * (1.0 / (math.sqrt(HBLK) * math.sqrt(mesh.size)))

    placed = (
        P(("inter", "intra"), None),
        P(("inter", "intra"), None),
        P("inter", "intra"),
        P("inter", None),
        P("inter", None),
        P(),
    )
    return jax.shard_map(
        body, mesh=mesh, in_specs=placed, out_specs=P("inter", None), check_vma=False
    )
```
